512 devices in a mesh: inp: 64 (over z, y), tblk: 8 (over x, core).
Axes of the slice: x: 4, y: 4, z: 16, core: 2. Of those that a mesh axis runs over, the one named last changes fastest.
Arguments:
- samples: bfloat16 [1024, 192, 2048], P('inp', 'tblk'), may hold values from -40 to 40
- kept: int32 [384], replicated, may hold values from 0 to 1023, as said below
Outputs:
- visibilities: bfloat16 [384, 2, 1024, 1024], P('inp', None, 'tblk')
The draws below stay inside these ranges and needn't reach their ends.
Inputs may be any that keep to these rules, and one draw needn't show every extreme that they name: `kept`: 384 distinct channel indices in increasing order; 0 and 1023 are always among them.
All inputs are finite; a program needn't handle non-finite values.
Results may differ from the reference program's by a relative error of at most 0.0042.
Values may be sent and summed in bfloat16 or wider, within the bound.
No kernel may reach another device: no remote copies, remote signals or barrier semaphores. Data moves between devices by JAX's collectives and lax.ppermute only.
A program may use at most 64 MiB of HBM per device.

```python
import math
import jax
import jax.numpy as jnp
from jax import lax

A = 1024
NCH = 1024
L = 2048
TAPS = 4
SPEC = 192
KEEP = 384
N_INP = 64


def draw_samples(key, part):
    key = jax.random.fold_in(key, 11)
    key_noise, key_sky, key_gain = jax.random.split(key, 3)
    noise = jnp.clip(jax.random.normal(key_noise, (A, SPEC, L), jnp.float32), -6.0, 6.0)
    sky = 0.5 * jnp.clip(jax.random.normal(key_sky, (SPEC, L), jnp.float32), -6.0, 6.0)
    gains = jnp.exp(jax.random.uniform(key_gain, (A,), jnp.float32, -0.7, 0.7))
    return (gains[:, None, None] * (noise + sky[None, :, :])).astype(jnp.bfloat16)


def draw_kept(key, part):
    key = jax.random.fold_in(key, 23)
    inner = jax.random.permutation(key, NCH - 2)[:KEEP - 2] + 1
    chosen = jnp.concatenate([jnp.array([0, NCH - 1], jnp.int32), inner.astype(jnp.int32)])
    return jnp.sort(chosen).astype(jnp.int32)


def setup_inputs(seed: int = 0) -> dict:
    arg_keys = jax.random.split(jax.random.key(seed), 3)
    return {
        "samples": draw_samples(jax.random.fold_in(arg_keys[2], 71), 0),
        "kept": draw_kept(jax.random.fold_in(arg_keys[2], 71), 0),
    }


def window_table(taps, length_total):
    span = taps * length_total
    m = jnp.arange(span, dtype=jnp.float32)
    proto = jnp.sinc((m - span / 2.0) / length_total) * (0.5 - 0.5 * jnp.cos(2.0 * math.pi * m / span))
    return proto.reshape(taps, length_total)[::-1]

def fourier_table(kept, length_total):
    current_position = jnp.arange(length_total, dtype=jnp.int32)
    phase = kept.astype(jnp.int32)[:, None] * current_position[None, :] % length_total
    angle = phase.astype(jnp.float32) * (2.0 * math.pi / length_total)
    return jnp.stack([jnp.cos(angle), -jnp.sin(angle)], axis=1).astype(jnp.bfloat16)

def reference(samples, kept):
    length_total = 2 * NCH
    group = A // N_INP
    weights = window_table(TAPS, length_total)
    table = fourier_table(kept, length_total).astype(jnp.float32)
    hp = lax.Precision.HIGHEST

    def channelize(block):
        sample_history = jnp.zeros((group, TAPS - 1, length_total), jnp.float32)
        extended_samples = jnp.concatenate([sample_history, block.astype(jnp.float32)], axis=1)
        filtered = jnp.zeros((group, SPEC, length_total), jnp.float32)
        for tap in range(TAPS):
            first = TAPS - 1 - tap
            filtered = filtered + weights[tap] * extended_samples[:, first:first + SPEC, :]
        filtered = filtered.astype(jnp.bfloat16).astype(jnp.float32)
        spec = jnp.einsum('cpn,isn->cpis', table, filtered, precision=hp)
        return (spec / math.sqrt(length_total)).astype(jnp.bfloat16)
    parts = lax.map(channelize, samples.reshape(N_INP, group, SPEC, length_total))
    spectra = jnp.transpose(parts, (1, 2, 0, 3, 4)).reshape(KEEP, 2, A, SPEC)

    def correlate_single(block):
        values = block.astype(jnp.float32)
        real_part = values[0]
        imag_part = values[1]
        vis_re = jnp.dot(real_part, real_part.T, precision=hp) + jnp.dot(imag_part, imag_part.T, precision=hp)
        vis_im = jnp.dot(imag_part, real_part.T, precision=hp) - jnp.dot(real_part, imag_part.T, precision=hp)
        return (jnp.stack([vis_re, vis_im], axis=0) / SPEC).astype(jnp.bfloat16)
    return lax.map(correlate_single, spectra)
```

```python
import math

import jax
import jax.numpy as jnp
from jax import lax
from jax.sharding import PartitionSpec as P

TAPS = 4


def from_behind(block, axis, distance):
    devices = range(lax.axis_size(axis))
    route = [(i - distance, i) for i in devices if i - distance in devices]
    return lax.ppermute(block, axis, route)


def window_table(taps, length_total):
    span = taps * length_total
    m = jnp.arange(span, dtype=jnp.float32)
    proto = jnp.sinc((m - span / 2.0) / length_total) * (
        0.5 - 0.5 * jnp.cos(2.0 * math.pi * m / span)
    )
    return proto.reshape(taps, length_total)[::-1]


def fourier_table(kept, length_total):
    lo = jnp.arange(128, dtype=jnp.int32)
    hi = jnp.arange(length_total // 128, dtype=jnp.int32) * 128
    step = 2.0 * math.pi / length_total
    a = (kept[:, None] * hi[None, :] % length_total).astype(jnp.float32) * step
    b = (kept[:, None] * lo[None, :] % length_total).astype(jnp.float32) * step
    ca, sa = jnp.cos(a)[:, :, None], jnp.sin(a)[:, :, None]
    cb, sb = jnp.cos(b)[:, None, :], jnp.sin(b)[:, None, :]
    re = (ca * cb - sa * sb).reshape(-1, length_total)
    im = -(sa * cb + ca * sb).reshape(-1, length_total)
    return jnp.stack([re, im], axis=1).astype(jnp.bfloat16)


def local(samples, kept):
    width_in, spd, length_total = samples.shape
    keep = kept.shape[0]
    groups = lax.axis_size("inp")
    count = lax.axis_size("tblk")
    block = lax.axis_index("tblk")
    sample_history = from_behind(samples[:, spd - (TAPS - 1) :, :], "tblk", 1)
    extended_samples = jnp.concatenate([sample_history, samples], axis=1)
    weights = window_table(TAPS, length_total)
    filtered = jnp.zeros((width_in, spd, length_total), jnp.float32)
    for tap in range(TAPS):
        first = TAPS - 1 - tap
        filtered = filtered + weights[tap] * extended_samples[:, first : first + spd, :].astype(
            jnp.float32
        )
    filtered = filtered.astype(jnp.bfloat16).reshape(width_in * spd, length_total)
    table = fourier_table(kept, length_total).reshape(2 * keep, length_total)
    spectra = jnp.einsum("kn,rn->kr", table, filtered, preferred_element_type=jnp.float32)
    spectra = (spectra / math.sqrt(length_total)).astype(jnp.bfloat16)
    own = keep // groups
    spectra = spectra.reshape(groups, own * 2, width_in * spd)
    owned = lax.all_to_all(spectra, "inp", split_axis=0, concat_axis=0, tiled=True)
    owned = owned.reshape(groups, own, 2, width_in, spd).transpose(1, 2, 4, 0, 3)
    owned = owned.reshape(own, 2 * spd, groups * width_in)
    whole = lax.all_gather(owned, "tblk", axis=0)
    whole = whole.reshape(count, own, 2, spd, groups * width_in)
    rows = groups * width_in // count
    picked = lax.dynamic_slice_in_dim(whole, block * rows, rows, 4)
    first = picked
    second = jnp.stack([picked[:, :, 1], -picked[:, :, 0]], axis=2)
    left = jnp.stack([first, second], axis=2)
    totals = jnp.einsum("tcypsh,tcpsa->cyha", left, whole, preferred_element_type=jnp.float32)
    return (totals / (spd * count)).astype(jnp.bfloat16)


def solution(mesh):
    placed = (P("inp", "tblk", None), P())
    return jax.shard_map(
        local, mesh=mesh, in_specs=placed, out_specs=P("inp", None, "tblk", None), check_vma=False
    )
```

```python
import math

import jax
import jax.numpy as jnp
from jax import lax
from jax.experimental import pallas as pl
from jax.experimental.pallas import tpu as pltpu
from jax.sharding import PartitionSpec as P

TAPS = 4
L = 2048
G = 64
C = 6
Q = 12
I = 16
S = 24
F32, BF16 = jnp.float32, jnp.bfloat16
PARAMS = pltpu.CompilerParams(vmem_limit_bytes=40 * 1024 * 1024)
VMEM = pl.BlockSpec(memory_space=pltpu.VMEM)


def dot(a, b, ca, cb):
    return lax.dot_general(a, b, (((ca,), (cb,)), ((), ())), preferred_element_type=F32)


def iota(shape, dim):
    return lax.broadcasted_iota(jnp.int32, shape, dim)


def window_table(taps, length_total):
    span = taps * length_total
    m = jnp.arange(span, dtype=F32)
    proto = jnp.sinc((m - span / 2.0) / length_total) * (
        0.5 - 0.5 * jnp.cos(2.0 * math.pi * m / span)
    )
    return proto.reshape(taps, length_total)[::-1]


def cosine(m):
    r = jnp.abs(((m + L // 2) & (L - 1)) - L // 2)
    flip = r > L // 4
    r = jnp.where(flip, L // 2 - r, r)
    u = r.astype(F32) * (2.0 * math.pi / L)
    u = u * u
    acc = jnp.full_like(u, 1.0 / math.factorial(14) * -1.0)
    for k in range(6, -1, -1):
        acc = acc * u + (-1.0) ** k / math.factorial(2 * k)
    return jnp.where(flip, -acc, acc)


def table_kernel(kept_ref, table_ref, swap_ref):
    rows = G * Q
    half = G * 8
    r = iota((rows, 1), 0)
    low = r - half
    flat_a = (r // 8) * Q + r % 8
    flat_b = ((low // 4) % 2 * (G // 2) + low // 8) * Q + 8 + low % 4
    flat = jnp.where(r < half, flat_a, flat_b)
    keep = kept_ref.shape[1]
    hit = iota((rows, keep), 1) == flat // 2
    chan = jnp.sum(jnp.where(hit, kept_ref[...].astype(F32), 0.0), axis=1, keepdims=True)
    chan = chan.astype(jnp.int32)
    lane = iota((rows, 128), 1)
    a = chan * lane * 128 + (flat % 2) * (L // 4)
    b = chan * lane
    ca, sa = cosine(a), cosine(a + 3 * (L // 4))
    cb, sb = cosine(b), cosine(b + 3 * (L // 4))
    for h in range(L // 128):
        part = ca[:, h : h + 1] * cb - sa[:, h : h + 1] * sb
        table_ref[:, h * 128 : (h + 1) * 128] = part.astype(BF16)
    n = 1024
    for h in range(n // 128):
        col = iota((n, 128), 1)
        want = (col // 16) * 128 + h * 16 + col % 16
        swap_ref[:, h * 128 : (h + 1) * 128] = jnp.where(iota((n, 128), 0) == want, 1.0, 0.0).astype(BF16)


def spectra_kernel(table_ref, samples_ref, halo_ref, weights_ref, out_ref, filtered):
    step = 512
    row = iota((8, step), 0)

    def fir(pair, carry):
        for n in range(0, L, step):
            cols = slice(n, n + step)
            parts = []
            for one in range(2):
                i = pair * 2 + one
                now = samples_ref[i, :, cols].astype(F32)
                back = halo_ref[i, :, cols].astype(F32)
                back = jnp.concatenate([back, back], axis=0)
                total = weights_ref[0:1, cols] * now
                for d in range(1, TAPS):
                    moved = pltpu.roll(now, d, 0)
                    head = jnp.where(row < d, pltpu.roll(back, d, 0), moved[0:8])
                    moved = jnp.concatenate([head, moved[8:]], axis=0)
                    total = total + weights_ref[d : d + 1, cols] * moved
                parts.append(total)
            both = jnp.concatenate(parts, axis=0).astype(BF16)
            filtered[pl.ds(pl.multiple_of(pair * 2 * S, 2 * S), 2 * S), cols] = both
        return carry

    lax.fori_loop(0, I // 2, fir, 0)
    width = I * S
    col = iota((width, width), 1)
    order = jnp.where(iota((width, width), 0) == (col % I) * S + col // I, 1.0, 0.0).astype(BF16)
    scale = 1.0 / math.sqrt(L)

    def transform(first):
        value = dot(table_ref[first : first + 256, :], filtered[...], 1, 1) * scale
        value = dot(value.astype(BF16), order, 1, 0)
        return value.reshape(32, 8, width)

    rest = transform(512)
    turned = pltpu.roll(rest, 4, 1)
    top = iota((32, 8, 128), 1) < 4
    for a in range(2):
        main = transform(a * 256)
        here, there = (rest, turned) if a == 0 else (turned, rest)
        owners = slice(a * 32, (a + 1) * 32)
        out_ref[owners, 0:16, :] = jnp.concatenate(
            [main[:, :, 0:128], main[:, :, 128:256]], axis=1
        ).astype(BF16)
        mixed = jnp.where(top, here[:, :, 0:128], there[:, :, 128:256])
        out_ref[owners, 16:32, :] = jnp.concatenate([main[:, :, 256:384], mixed], axis=1).astype(BF16)
        out_ref[owners, 32:36, :] = here[:, 0:4, 256:384].astype(BF16)


def regroup_kernel(owned_ref, swap_ref, out_ref, rows_ref, wide_ref):
    units = 36
    for g in range(G):
        big, small = g // 8, g % 8
        rows_ref[big * 48 : big * 48 + units, small * 128 : (small + 1) * 128] = owned_ref[g]
    for s in range(8):
        wide_ref[s * 40 + 32 : s * 40 + 40, :] = jnp.zeros((8, 1024), F32)
    for h in range(4):
        cols = slice(h * 256, (h + 1) * 256)
        part = dot(rows_ref[...], swap_ref[:, cols], 1, 0)
        for big in range(8):
            for s in range(2):
                place = (h * 2 + s) * 40
                wide_ref[place : place + units, big * 128 : (big + 1) * 128] = part[
                    big * 48 : big * 48 + units, s * 128 : (s + 1) * 128
                ]
    shape = (Q * S, 320)
    r = iota(shape, 0)
    q, s = r // S, r % S
    third = s // 8
    unit = jnp.where(q < 8, third * 8 + q, 24 + third * 4 + q - 8)
    order = jnp.where(iota(shape, 1) == (s % 8) * 40 + unit, 1.0, 0.0).astype(BF16)
    out_ref[...] = dot(order, wide_ref[...].astype(BF16), 1, 0).astype(BF16)


def correlate_kernel(block_ref, *refs):
    blocks, out_ref = refs[:-1], refs[-1]
    c = pl.program_id(0)
    early = c < C // 2
    first = pl.multiple_of(block_ref[0] * 128, 128)
    right, left = [], []
    for half in range(2):
        own, up, down, far_a, far_b = blocks[half * 5 : half * 5 + 5]
        for ref in (own, up, down):
            right.append(ref[...])
            left.append(ref[:, pl.ds(first, 128)].astype(F32))
        right.append(jnp.where(early, far_a[...], far_b[...]))
        left.append(
            jnp.where(early, far_a[:, pl.ds(first, 128)].astype(F32), far_b[:, pl.ds(first, 128)].astype(F32))
        )
    right = jnp.concatenate(right, axis=0)
    other = [jnp.concatenate([v[S:], -v[:S]], axis=0) for v in left]
    left = jnp.concatenate([jnp.concatenate(left, axis=0), jnp.concatenate(other, axis=0)], axis=1)
    total = dot(left.astype(BF16), right, 0, 0) * (1.0 / (8 * S))
    out_ref[0] = total.reshape(2, 128, 1024).astype(BF16)


def local(samples, kept):
    block = lax.axis_index("tblk")
    steps = lax.axis_size("tblk")
    halo = lax.ppermute(samples[:, S - 4 :, :], "tblk", [(i, i + 1) for i in range(steps - 1)])
    weights = window_table(TAPS, L)
    table, swap = pl.pallas_call(
        table_kernel,
        out_shape=[
            jax.ShapeDtypeStruct((G * Q, L), BF16),
            jax.ShapeDtypeStruct((1024, 1024), BF16),
        ],
        in_specs=[VMEM],
        out_specs=[VMEM, VMEM],
        compiler_params=PARAMS,
        cost_estimate=pl.CostEstimate(flops=10_000_000, bytes_accessed=5_000_000, transcendentals=0),
    )(kept.reshape(1, -1))
    chunks = pl.pallas_call(
        spectra_kernel,
        out_shape=jax.ShapeDtypeStruct((G, 36, 128), BF16),
        in_specs=[VMEM] * 4,
        out_specs=VMEM,
        scratch_shapes=[pltpu.VMEM((I * S, L), BF16)],
        compiler_params=PARAMS,
    )(table, samples, halo, weights)
    owned = lax.all_to_all(chunks, "inp", split_axis=0, concat_axis=0, tiled=True)
    mine = pl.pallas_call(
        regroup_kernel,
        out_shape=jax.ShapeDtypeStruct((Q * S, 1024), BF16),
        in_specs=[VMEM] * 2,
        out_specs=VMEM,
        scratch_shapes=[pltpu.VMEM((384, 1024), BF16), pltpu.VMEM((320, 1024), F32)],
        compiler_params=PARAMS,
    )(owned, swap)
    core = [(i, i ^ 1) for i in range(steps)]
    plus = [(i, (i + 2) % steps) for i in range(steps)]
    minus = [(i, (i - 2) % steps) for i in range(steps)]
    send = lambda v, route: lax.ppermute(v, "tblk", route)
    up, down = send(mine, plus), send(mine, minus)
    mine_o = send(mine, core)
    mid = Q * S // 2
    far_a, far_b = send(up[:mid], plus), send(down[mid:], minus)
    up_o, down_o = send(up, core), send(down, core)
    far_ao, far_bo = send(far_a, core), send(far_b, core)
    near = pl.BlockSpec((2 * S, 1024), lambda c, b: (c, 0))
    head = pl.BlockSpec((2 * S, 1024), lambda c, b: (jnp.minimum(c, 2), 0))
    tail = pl.BlockSpec((2 * S, 1024), lambda c, b: (jnp.maximum(c - 3, 0), 0))
    specs = [near, near, near, head, tail] * 2
    return pl.pallas_call(
        correlate_kernel,
        out_shape=jax.ShapeDtypeStruct((C, 2, 128, 1024), BF16),
        grid_spec=pltpu.PrefetchScalarGridSpec(
            num_scalar_prefetch=1,
            grid=(C,),
            in_specs=specs,
            out_specs=pl.BlockSpec((1, 2, 128, 1024), lambda c, b: (c, 0, 0, 0)),
        ),
        compiler_params=PARAMS,
    )(block.reshape(1), mine, up, down, far_a, far_b, mine_o, up_o, down_o, far_ao, far_bo)


def solution(mesh):
    placed = (P("inp", "tblk", None), P())
    return jax.shard_map(
        local, mesh=mesh, in_specs=placed, out_specs=P("inp", None, "tblk", None), check_vma=False
    )
```

```python
import math

import jax
import jax.numpy as jnp
from jax import lax
from jax.experimental import pallas as pl
from jax.experimental.pallas import tpu as pltpu
from jax.sharding import PartitionSpec as P

TAPS = 4
L = 2048
G = 64
C = 6
Q = 12
I = 16
S = 24
F32, BF16 = jnp.float32, jnp.bfloat16
PARAMS = pltpu.CompilerParams(vmem_limit_bytes=24 * 1024 * 1024)
VMEM = pl.BlockSpec(memory_space=pltpu.VMEM)


def dot(a, b, ca, cb):
    return lax.dot_general(a, b, (((ca,), (cb,)), ((), ())), preferred_element_type=F32)


def iota(shape, dim):
    return lax.broadcasted_iota(jnp.int32, shape, dim)


def window_table(taps, length_total):
    span = taps * length_total
    t = lax.broadcasted_iota(F32, (taps, length_total), 0)
    m = (taps - 1 - t) * length_total + lax.broadcasted_iota(F32, (taps, length_total), 1)
    return jnp.sinc((m - span / 2.0) / length_total) * (
        0.5 - 0.5 * jnp.cos(2.0 * math.pi * m / span)
    )


def cosine(m):
    r = jnp.abs(((m + L // 2) & (L - 1)) - L // 2)
    flip = r > L // 4
    r = jnp.where(flip, L // 2 - r, r)
    u = r.astype(F32) * (2.0 * math.pi / L)
    u = u * u
    acc = jnp.full_like(u, 1.0 / math.factorial(14) * -1.0)
    for k in range(6, -1, -1):
        acc = acc * u + (-1.0) ** k / math.factorial(2 * k)
    return jnp.where(flip, -acc, acc)


def tail_kernel(samples_ref, out_ref):
    out_ref[...] = samples_ref[:, S - 8 :, :].astype(F32)[:, 4:, :].astype(BF16)


def table_kernel(kept_ref, table_ref, swap_ref):
    rows = 2 * G * 4
    r = iota((rows, 1), 0)
    owner = (r // 4) % 2 * (G // 2) + (r // 8) % 32
    tail = r >= G * 4
    want = owner * C + jnp.where(tail, 4 + r % 2, r % 4)
    keep = kept_ref.shape[0]
    chan = jnp.sum(
        jnp.where(iota((rows, keep), 1) == want, kept_ref[...].astype(F32).reshape(1, keep), 0.0), axis=1, keepdims=True
    ).astype(jnp.int32)
    turn = jnp.where(tail, (r // 2) % 2 * (L // 4), 0)
    lane = iota((rows, 128), 1)
    step = chan * 128
    cs = cosine(step + jnp.where(lane < 64, 0, 3 * (L // 4)))
    first = chan * lane + turn
    re0, im0 = cosine(first), cosine(first + 3 * (L // 4))
    half = G * 4
    for n in range(0, rows, 64):
        at = slice(n, n + 64)
        re, im = re0[at], im0[at]
        ca, sa = jnp.broadcast_to(cs[at, 0:1], (64, 128)), jnp.broadcast_to(cs[at, 64:65], (64, 128))
        place = n if n < half else n + half
        for h in range(L // 128):
            cols = slice(h * 128, (h + 1) * 128)
            table_ref[place : place + 64, cols] = re.astype(BF16)
            if n < half:
                table_ref[half + n : half + n + 64, cols] = (-im).astype(BF16)
            re, im = re * ca - im * sa, re * sa + im * ca
    n = 1024
    col = iota((1, 128), 1)
    base = iota((n, 128), 0) - ((col // 16) * 128 + col % 16)
    for h in range(n // 128):
        swap_ref[:, h * 128 : (h + 1) * 128] = jnp.where(base == h * 16, 1.0, 0.0).astype(BF16)


def spectra_kernel(table_ref, samples_ref, halo_ref, weights_ref, out_ref, filtered):
    step = 512
    row = iota((8, step), 0)

    def fir(pair, carry):
        for n in range(0, L, step):
            cols = slice(n, n + step)
            parts = []
            for one in range(2):
                i = pair * 2 + one
                now = samples_ref[i, :, cols].astype(F32)
                back = halo_ref[i, :, cols].astype(F32)
                back = jnp.concatenate([back, back], axis=0)
                total = weights_ref[0:1, cols] * now
                for d in range(1, TAPS):
                    moved = pltpu.roll(now, d, 0)
                    head = jnp.where(row < d, pltpu.roll(back, d, 0), moved[0:8])
                    moved = jnp.concatenate([head, moved[8:]], axis=0)
                    total = total + weights_ref[d : d + 1, cols] * moved
                parts.append(total)
            both = jnp.concatenate(parts, axis=0).astype(BF16)
            filtered[pl.ds(pl.multiple_of(pair * 2 * S, 2 * S), 2 * S), cols] = both
        return carry

    lax.fori_loop(0, I // 2, fir, 0)
    width = I * S
    col = iota((width, width), 1)
    order = jnp.where(iota((width, width), 0) == (col % I) * S + col // I, 1.0, 0.0).astype(BF16)
    scale = 1.0 / math.sqrt(L)

    def transform(first):
        value = dot(table_ref[first : first + 256, :], filtered[...], 1, 1) * scale
        value = dot(value.astype(BF16), order, 1, 0)
        return value.reshape(32, 8, width)

    for m in range(3):
        value = transform(m * 256).astype(BF16)
        out_ref[0:32, :, m * width : (m + 1) * width] = value[:, 0:4]
        out_ref[32:64, :, m * width : (m + 1) * width] = value[:, 4:8]


def regroup_kernel(owned_ref, swap_ref, all_ref, low_ref, high_ref, rows_ref, wide_ref):
    units = 36
    for g in range(G):
        big, small = g // 8, g % 8
        for t in range(9):
            place = big * 40 + t * 4
            rows_ref[place : place + 4, small * 128 : (small + 1) * 128] = owned_ref[
                g, :, t * 128 : (t + 1) * 128
            ].astype(F32)
    for s in range(8):
        wide_ref[s * 40 + 32 : s * 40 + 40, :] = jnp.zeros((8, 1024), F32)
    rows = rows_ref[...].astype(BF16)
    for h in range(4):
        part = dot(rows, swap_ref[:, h * 256 : (h + 1) * 256], 1, 0)
        for big in range(8):
            for s in range(2):
                place = (h * 2 + s) * 40
                wide_ref[place : place + units, big * 128 : (big + 1) * 128] = part[
                    big * 40 : big * 40 + units, s * 128 : (s + 1) * 128
                ]
    shape = (Q * S, 320)
    r = iota(shape, 0)
    q, s = r // S, r % S
    c, p = q // 2, q % 2
    m = jnp.where(c < 4, p, 2)
    unit = (m * 3 + s // 8) * 4 + jnp.where(c < 4, c, p * 2 + c - 4)
    order = jnp.where(iota(shape, 1) == (s % 8) * 40 + unit, 1.0, 0.0).astype(BF16)
    mine = dot(order, wide_ref[...].astype(BF16), 1, 0).astype(BF16)
    all_ref[...] = mine
    low_ref[...] = mine[: Q * S // 2]
    high_ref[...] = mine[Q * S // 2 :]


PER = C // 2


def correlate_kernel(block_ref, *refs):
    mine, up_low, down_low, far_low, up_high, down_high, far_high, first_o, last_o, out_ref = refs
    first = pl.multiple_of(block_ref[0] * 128, 128)
    depth = 2 * S
    mid = PER * depth

    def run(places):
        for one in range(PER):
            left, other, right = [], [], []
            for ref, base in places:
                rows = slice(base + one * depth, base + (one + 1) * depth)
                v = ref[rows, pl.ds(first, 128)].astype(F32)
                left.append(v)
                other += [v[S:], -v[:S]]
                right.append(ref[rows, :])
            right = jnp.concatenate(right, axis=0)
            left = jnp.concatenate(
                [jnp.concatenate(left, axis=0), jnp.concatenate(other, axis=0)], axis=1
            )
            total = dot(left.astype(BF16), right, 0, 0) * (1.0 / (8 * S))
            out_ref[one] = total.reshape(2, 128, 1024).astype(BF16)

    @pl.when(pl.program_id(0) == 0)
    def _():
        run([(mine, 0), (up_low, 0), (down_low, 0), (far_low, 0)]
            + [(first_o, 0), (first_o, 2 * mid), (last_o, 0), (last_o, 2 * mid)])

    @pl.when(pl.program_id(0) == 1)
    def _():
        run([(mine, mid), (up_high, 0), (down_high, 0), (far_high, 0)]
            + [(first_o, mid), (first_o, 3 * mid), (last_o, mid), (last_o, 3 * mid)])


def local(samples, kept):
    block = lax.axis_index("tblk").reshape(1)
    steps = lax.axis_size("tblk")
    tail = pl.pallas_call(
        tail_kernel,
        out_shape=jax.ShapeDtypeStruct((I, 4, L), BF16),
        in_specs=[VMEM],
        out_specs=VMEM,
        compiler_params=PARAMS,
    )(samples)
    halo = lax.ppermute(tail, "tblk", [(i, i + 1) for i in range(steps - 1)])
    weights = window_table(TAPS, L)
    table, swap = pl.pallas_call(
        table_kernel,
        out_shape=[
            jax.ShapeDtypeStruct((G * Q, L), BF16),
            jax.ShapeDtypeStruct((1024, 1024), BF16),
        ],
        in_specs=[VMEM],
        out_specs=[VMEM, VMEM],
        compiler_params=PARAMS,
        cost_estimate=pl.CostEstimate(flops=10_000_000, bytes_accessed=20_000_000, transcendentals=0),
    )(kept)
    chunks = pl.pallas_call(
        spectra_kernel,
        out_shape=jax.ShapeDtypeStruct((G, 4, 1152), BF16),
        in_specs=[VMEM] * 4,
        out_specs=VMEM,
        scratch_shapes=[pltpu.VMEM((I * S, L), BF16)],
        compiler_params=PARAMS,
    )(table, samples, halo, weights)
    owned = lax.all_to_all(chunks, "inp", split_axis=0, concat_axis=0, tiled=True)
    rows = Q * S
    mine, low, high = pl.pallas_call(
        regroup_kernel,
        out_shape=[jax.ShapeDtypeStruct((n, 1024), BF16) for n in (rows, rows // 2, rows // 2)],
        in_specs=[VMEM] * 2,
        out_specs=[VMEM] * 3,
        scratch_shapes=[pltpu.VMEM((320, 1024), F32), pltpu.VMEM((320, 1024), F32)],
        compiler_params=PARAMS,
    )(owned, swap)
    send = lambda v, hop: lax.ppermute(v, "tblk", [(i, (i + hop) % steps) for i in range(steps)])
    flip = lambda *v: lax.ppermute(
        jnp.concatenate(v, axis=0), "tblk", [(i, i ^ 1) for i in range(steps)]
    )
    up_low, down_high = send(low, 2), send(high, -2)
    up_high, down_low = send(high, 2), send(low, -2)
    far_low, far_high = send(up_low, 2), send(down_high, -2)
    first_o = flip(mine, up_low, down_high)
    last_o = flip(down_low, up_high, far_low, far_high)
    return pl.pallas_call(
        correlate_kernel,
        out_shape=jax.ShapeDtypeStruct((C, 2, 128, 1024), BF16),
        grid_spec=pltpu.PrefetchScalarGridSpec(
            num_scalar_prefetch=1,
            grid=(C // PER,),
            in_specs=[VMEM] * 9,
            out_specs=pl.BlockSpec((PER, 2, 128, 1024), lambda c, b: (c, 0, 0, 0)),
        ),
        compiler_params=PARAMS,
    )(block, mine, up_low, down_low, far_low, up_high, down_high, far_high, first_o, last_o)


def solution(mesh):
    placed = (P("inp", "tblk", None), P())
    return jax.shard_map(
        local, mesh=mesh, in_specs=placed, out_specs=P("inp", None, "tblk", None), check_vma=False
    )
```

```python
import math

import jax
import jax.numpy as jnp
from jax import lax
from jax.experimental import pallas as pl
from jax.experimental.pallas import tpu as pltpu
from jax.sharding import PartitionSpec as P

TAPS = 4
L = 2048
G = 64
C = 6
Q = 12
I = 16
S = 24
F32, BF16 = jnp.float32, jnp.bfloat16
PARAMS = pltpu.CompilerParams(vmem_limit_bytes=16 * 1024 * 1024)
VMEM = pl.BlockSpec(memory_space=pltpu.VMEM)


def dot(a, b, ca, cb):
    return lax.dot_general(a, b, (((ca,), (cb,)), ((), ())), preferred_element_type=F32)


def iota(shape, dim):
    return lax.broadcasted_iota(jnp.int32, shape, dim)


def window_table(taps, length_total):
    span = taps * length_total
    t = lax.broadcasted_iota(F32, (taps, length_total), 0)
    m = (taps - 1 - t) * length_total + lax.broadcasted_iota(F32, (taps, length_total), 1)
    return jnp.sinc((m - span / 2.0) / length_total) * (
        0.5 - 0.5 * jnp.cos(2.0 * math.pi * m / span)
    )


def cosine(m):
    r = jnp.abs(((m + L // 2) & (L - 1)) - L // 2)
    flip = r > L // 4
    r = jnp.where(flip, L // 2 - r, r)
    u = r.astype(F32) * (2.0 * math.pi / L)
    u = u * u
    acc = jnp.full_like(u, 1.0 / math.factorial(14) * -1.0)
    for k in range(6, -1, -1):
        acc = acc * u + (-1.0) ** k / math.factorial(2 * k)
    return jnp.where(flip, -acc, acc)


def tail_kernel(samples_ref, kept_ref, out_ref, kept_out):
    out_ref[...] = samples_ref[:, S - 8 :, :].astype(F32)[:, 4:, :].astype(BF16)
    kept_out[...] = kept_ref[...].astype(F32).reshape(1, kept_ref.shape[0])


def table_kernel(kept_ref, table_ref, swap_ref):
    rows = 2 * G * 4
    r = iota((rows, 1), 0)
    owner = (r // 4) % 2 * (G // 2) + (r // 8) % 32
    tail = r >= G * 4
    want = owner * C + jnp.where(tail, 4 + r % 2, r % 4)
    keep = kept_ref.shape[1]
    chan = jnp.sum(
        jnp.where(iota((rows, keep), 1) == want, kept_ref[...], 0.0), axis=1, keepdims=True
    ).astype(jnp.int32)
    turn = jnp.where(tail, (r // 2) % 2 * (L // 4), 0)
    lane = iota((rows, 128), 1)
    step = chan * 128
    cs = cosine(step + jnp.where(lane < 64, 0, 3 * (L // 4)))
    first = chan * lane + turn
    re0, im0 = cosine(first), cosine(first + 3 * (L // 4))
    half = G * 4
    for n in range(0, rows, 64):
        at = slice(n, n + 64)
        re, im = re0[at], im0[at]
        ca, sa = jnp.broadcast_to(cs[at, 0:1], (64, 128)), jnp.broadcast_to(cs[at, 64:65], (64, 128))
        place = n if n < half else n + half
        for h in range(L // 128):
            cols = slice(h * 128, (h + 1) * 128)
            table_ref[place : place + 64, cols] = re.astype(BF16)
            if n < half:
                table_ref[half + n : half + n + 64, cols] = (-im).astype(BF16)
            re, im = re * ca - im * sa, re * sa + im * ca
    n = 1024
    col = iota((1, 128), 1)
    base = iota((n, 128), 0) - ((col // 16) * 128 + col % 16)
    for h in range(n // 128):
        swap_ref[:, h * 128 : (h + 1) * 128] = jnp.where(base == h * 16, 1.0, 0.0).astype(BF16)


def spectra_kernel(table_ref, samples_ref, halo_ref, weights_ref, out_ref, filtered):
    step = 512
    row = iota((8, step), 0)

    def fir(pair, carry):
        for n in range(0, L, step):
            cols = slice(n, n + step)
            parts = []
            for one in range(2):
                i = pair * 2 + one
                now = samples_ref[i, :, cols].astype(F32)
                back = halo_ref[i, :, cols].astype(F32)
                back = jnp.concatenate([back, back], axis=0)
                total = weights_ref[0:1, cols] * now
                for d in range(1, TAPS):
                    moved = pltpu.roll(now, d, 0)
                    head = jnp.where(row < d, pltpu.roll(back, d, 0), moved[0:8])
                    moved = jnp.concatenate([head, moved[8:]], axis=0)
                    total = total + weights_ref[d : d + 1, cols] * moved
                parts.append(total)
            both = jnp.concatenate(parts, axis=0).astype(BF16)
            filtered[pl.ds(pl.multiple_of(pair * 2 * S, 2 * S), 2 * S), cols] = both
        return carry

    lax.fori_loop(0, I // 2, fir, 0)
    width = I * S
    col = iota((width, width), 1)
    order = jnp.where(iota((width, width), 0) == (col % I) * S + col // I, 1.0, 0.0).astype(BF16)
    scale = 1.0 / math.sqrt(L)

    def transform(first):
        value = dot(table_ref[first : first + 256, :], filtered[...], 1, 1) * scale
        value = dot(value.astype(BF16), order, 1, 0)
        return value.reshape(32, 8, width)

    for m in range(3):
        value = transform(m * 256).astype(BF16)
        out_ref[0:32, :, m * width : (m + 1) * width] = value[:, 0:4]
        out_ref[32:64, :, m * width : (m + 1) * width] = value[:, 4:8]


def regroup_kernel(owned_ref, swap_ref, all_ref, low_ref, high_ref, rows_ref, wide_ref):
    units = 36
    for g in range(G):
        big, small = g // 8, g % 8
        for t in range(9):
            place = big * 40 + t * 4
            rows_ref[place : place + 4, small * 128 : (small + 1) * 128] = owned_ref[
                g, :, t * 128 : (t + 1) * 128
            ].astype(F32)
    for s in range(8):
        wide_ref[s * 40 + 32 : s * 40 + 40, :] = jnp.zeros((8, 1024), F32)
    rows = rows_ref[...].astype(BF16)
    for h in range(4):
        part = dot(rows, swap_ref[:, h * 256 : (h + 1) * 256], 1, 0)
        for big in range(8):
            for s in range(2):
                place = (h * 2 + s) * 40
                wide_ref[place : place + units, big * 128 : (big + 1) * 128] = part[
                    big * 40 : big * 40 + units, s * 128 : (s + 1) * 128
                ]
    shape = (Q * S, 320)
    r = iota(shape, 0)
    q, s = r // S, r % S
    c, p = q // 2, q % 2
    m = jnp.where(c < 4, p, 2)
    unit = (m * 3 + s // 8) * 4 + jnp.where(c < 4, c, p * 2 + c - 4)
    order = jnp.where(iota(shape, 1) == (s % 8) * 40 + unit, 1.0, 0.0).astype(BF16)
    mine = dot(order, wide_ref[...].astype(BF16), 1, 0).astype(BF16)
    all_ref[...] = mine
    low_ref[...] = mine[: Q * S // 2]
    high_ref[...] = mine[Q * S // 2 :]


MID = C // 2
DEPTH = 2 * S


def products(first, places, one):
    left, other, right = [], [], []
    for ref, base in places:
        rows = slice(base + one * DEPTH, base + (one + 1) * DEPTH)
        v = ref[rows, pl.ds(first, 128)].astype(F32)
        left.append(v)
        other += [v[S:], -v[:S]]
        right.append(ref[rows, :])
    left = jnp.concatenate([jnp.concatenate(left, axis=0), jnp.concatenate(other, axis=0)], axis=1)
    return dot(left.astype(BF16), jnp.concatenate(right, axis=0), 0, 0) * (1.0 / (8 * S))


def places(first, last, high):
    half = MID * DEPTH
    at = half if high else 0
    return [(first, at), (first, 2 * half + at), (last, at), (last, 2 * half + at)]


def pack_kernel(*refs):
    at = 0
    for ref in refs[:-1]:
        refs[-1][at : at + ref.shape[0]] = ref[...]
        at += ref.shape[0]


def own_kernel(block_ref, first_ref, last_ref, out_ref):
    first = pl.multiple_of(block_ref[0] * 128, 128)
    for c in range(C):
        out_ref[c] = products(first, places(first_ref, last_ref, c >= MID), c % MID)


def other_kernel(block_ref, first_ref, last_ref, part_ref, out_ref):
    first = pl.multiple_of(block_ref[0] * 128, 128)
    for high in range(2):

        @pl.when(pl.program_id(0) == high)
        def _():
            for one in range(MID):
                total = products(first, places(first_ref, last_ref, high), one)
                total = total + part_ref[high * MID + one]
                out_ref[one] = total.reshape(2, 128, 1024).astype(BF16)


def local(samples, kept):
    block = lax.axis_index("tblk").reshape(1)
    steps = lax.axis_size("tblk")
    tail, channels = pl.pallas_call(
        tail_kernel,
        out_shape=[jax.ShapeDtypeStruct((I, 4, L), BF16), jax.ShapeDtypeStruct((1, kept.shape[0]), F32)],
        in_specs=[VMEM] * 2,
        out_specs=[VMEM] * 2,
        compiler_params=PARAMS,
    )(samples, kept)
    halo = lax.ppermute(tail, "tblk", [(i, i + 1) for i in range(steps - 1)])
    weights = window_table(TAPS, L)
    table, swap = pl.pallas_call(
        table_kernel,
        out_shape=[
            jax.ShapeDtypeStruct((G * Q, L), BF16),
            jax.ShapeDtypeStruct((1024, 1024), BF16),
        ],
        in_specs=[VMEM],
        out_specs=[VMEM, VMEM],
        compiler_params=PARAMS,
        cost_estimate=pl.CostEstimate(flops=10_000_000, bytes_accessed=20_000_000, transcendentals=0),
    )(channels)
    chunks = pl.pallas_call(
        spectra_kernel,
        out_shape=jax.ShapeDtypeStruct((G, 4, 1152), BF16),
        in_specs=[VMEM] * 4,
        out_specs=VMEM,
        scratch_shapes=[pltpu.VMEM((I * S, L), BF16)],
        compiler_params=PARAMS,
    )(table, samples, halo, weights)
    owned = lax.all_to_all(chunks, "inp", split_axis=0, concat_axis=0, tiled=True)
    rows = Q * S
    mine, low, high = pl.pallas_call(
        regroup_kernel,
        out_shape=[jax.ShapeDtypeStruct((n, 1024), BF16) for n in (rows, rows // 2, rows // 2)],
        in_specs=[VMEM] * 2,
        out_specs=[VMEM] * 3,
        scratch_shapes=[pltpu.VMEM((320, 1024), F32), pltpu.VMEM((320, 1024), F32)],
        compiler_params=PARAMS,
    )(owned, swap)
    send = lambda v, hop: lax.ppermute(v, "tblk", [(i, (i + hop) % steps) for i in range(steps)])
    flip = lambda v: lax.ppermute(v, "tblk", [(i, i ^ 1) for i in range(steps)])

    def pack(*parts):
        return pl.pallas_call(
            pack_kernel,
            out_shape=pltpu.VMEM((2 * rows, 1024), BF16),
            in_specs=[VMEM] * len(parts),
            out_specs=VMEM,
            compiler_params=PARAMS,
        )(*parts)

    up_low, down_high = send(low, 2), send(high, -2)
    up_high, down_low = send(high, 2), send(low, -2)
    far_low, far_high = send(up_low, 2), send(down_high, -2)
    near = pack(mine, up_low, down_high)
    near_o = flip(near)
    rest = pack(down_low, up_high, far_low, far_high)
    rest_o = flip(rest)
    part = pl.pallas_call(
        own_kernel,
        out_shape=pltpu.VMEM((C, 256, 1024), F32),
        in_specs=[pl.BlockSpec(memory_space=pltpu.SMEM)] + [VMEM] * 2,
        out_specs=VMEM,
        compiler_params=PARAMS,
        cost_estimate=pl.CostEstimate(flops=600_000_000, bytes_accessed=9_000_000, transcendentals=0),
    )(block, near, rest)
    return pl.pallas_call(
        other_kernel,
        out_shape=jax.ShapeDtypeStruct((C, 2, 128, 1024), BF16),
        grid_spec=pltpu.PrefetchScalarGridSpec(
            num_scalar_prefetch=1,
            grid=(2,),
            in_specs=[VMEM] * 3,
            out_specs=pl.BlockSpec((MID, 2, 128, 1024), lambda c, b: (c, 0, 0, 0)),
        ),
        compiler_params=PARAMS,
    )(block, near_o, rest_o, part)


def solution(mesh):
    placed = (P("inp", "tblk", None), P())
    return jax.shard_map(
        local, mesh=mesh, in_specs=placed, out_specs=P("inp", None, "tblk", None), check_vma=False
    )
```

```python
import math

import jax
import jax.numpy as jnp
from jax import lax
from jax.experimental import pallas as pl
from jax.experimental.pallas import tpu as pltpu
from jax.sharding import PartitionSpec as P

TAPS = 4
L = 2048
G = 64
C = 6
Q = 12
I = 16
S = 24
F32, BF16 = jnp.float32, jnp.bfloat16
PARAMS = pltpu.CompilerParams(vmem_limit_bytes=16 * 1024 * 1024)
VMEM = pl.BlockSpec(memory_space=pltpu.VMEM)


def dot(a, b, ca, cb):
    return lax.dot_general(a, b, (((ca,), (cb,)), ((), ())), preferred_element_type=F32)


def iota(shape, dim):
    return lax.broadcasted_iota(jnp.int32, shape, dim)


def window_table(taps, length_total):
    span = taps * length_total
    t = lax.broadcasted_iota(F32, (taps, length_total), 0)
    m = (taps - 1 - t) * length_total + lax.broadcasted_iota(F32, (taps, length_total), 1)
    return jnp.sinc((m - span / 2.0) / length_total) * (
        0.5 - 0.5 * jnp.cos(2.0 * math.pi * m / span)
    )


def cosine(m):
    r = jnp.abs(((m + L // 2) & (L - 1)) - L // 2)
    flip = r > L // 4
    r = jnp.where(flip, L // 2 - r, r)
    u = r.astype(F32) * (2.0 * math.pi / L)
    u = u * u
    acc = jnp.full_like(u, 1.0 / math.factorial(14) * -1.0)
    for k in range(6, -1, -1):
        acc = acc * u + (-1.0) ** k / math.factorial(2 * k)
    return jnp.where(flip, -acc, acc)


def tail_kernel(samples_ref, kept_ref, out_ref, kept_out):
    out_ref[...] = samples_ref[:, S - 8 :, :].astype(F32)[:, 4:, :].astype(BF16)
    kept_out[...] = kept_ref[...].astype(F32).reshape(1, kept_ref.shape[0])


def table_kernel(kept_ref, table_ref, swap_ref):
    rows = 2 * G * 4
    r = iota((rows, 1), 0)
    owner = (r // 4) % 2 * (G // 2) + (r // 8) % 32
    tail = r >= G * 4
    want = owner * C + jnp.where(tail, 4 + r % 2, r % 4)
    keep = kept_ref.shape[1]
    chan = jnp.sum(
        jnp.where(iota((rows, keep), 1) == want, kept_ref[...], 0.0), axis=1, keepdims=True
    ).astype(jnp.int32)
    turn = jnp.where(tail, (r // 2) % 2 * (L // 4), 0)
    lane = iota((rows, 128), 1)
    step = chan * 128
    cs = cosine(step + jnp.where(lane < 64, 0, 3 * (L // 4)))
    first = chan * lane + turn
    re0, im0 = cosine(first), cosine(first + 3 * (L // 4))
    half = G * 4
    for n in range(0, rows, 64):
        at = slice(n, n + 64)
        re, im = re0[at], im0[at]
        ca, sa = jnp.broadcast_to(cs[at, 0:1], (64, 128)), jnp.broadcast_to(cs[at, 64:65], (64, 128))
        place = n if n < half else n + half
        for h in range(L // 128):
            cols = slice(h * 128, (h + 1) * 128)
            table_ref[place : place + 64, cols] = re.astype(BF16)
            if n < half:
                table_ref[half + n : half + n + 64, cols] = (-im).astype(BF16)
            re, im = re * ca - im * sa, re * sa + im * ca
    n = 1024
    col = iota((1, 128), 1)
    base = iota((n, 128), 0) - ((col // 16) * 128 + col % 16)
    for h in range(n // 128):
        swap_ref[:, h * 128 : (h + 1) * 128] = jnp.where(base == h * 16, 1.0, 0.0).astype(BF16)


def spectra_kernel(table_ref, samples_ref, halo_ref, weights_ref, out_ref, filtered):
    step = 512

    def fir(pair, carry):
        for n in range(0, L, step):
            cols = slice(n, n + step)
            parts = []
            for one in range(2):
                i = pair * 2 + one
                now = samples_ref[i, :, cols].astype(F32)
                back = halo_ref[i, :, cols].astype(F32)
                frames = jnp.concatenate([back, back, now], axis=0)
                total = weights_ref[0:1, cols] * now
                for d in range(1, TAPS):
                    total = total + weights_ref[d : d + 1, cols] * pltpu.roll(frames, d, 0)[8:]
                parts.append(total)
            both = jnp.concatenate(parts, axis=0).astype(BF16)
            filtered[pl.ds(pl.multiple_of(pair * 2 * S, 2 * S), 2 * S), cols] = both
        return carry

    lax.fori_loop(0, I // 2, fir, 0)
    width = I * S
    col = iota((width, width), 1)
    order = jnp.where(iota((width, width), 0) == (col % I) * S + col // I, 1.0, 0.0).astype(BF16)
    scale = 1.0 / math.sqrt(L)

    def transform(first):
        value = dot(table_ref[first : first + 256, :], filtered[...], 1, 1) * scale
        value = dot(value.astype(BF16), order, 1, 0)
        return value.reshape(32, 8, width)

    for m in range(3):
        value = transform(m * 256).astype(BF16)
        out_ref[0:32, :, m * width : (m + 1) * width] = value[:, 0:4]
        out_ref[32:64, :, m * width : (m + 1) * width] = value[:, 4:8]


def regroup_kernel(owned_ref, swap_ref, all_ref, low_ref, high_ref, rows_ref, wide_ref):
    units = 36
    for g in range(G):
        big, small = g // 8, g % 8
        for t in range(9):
            place = big * 40 + t * 4
            rows_ref[place : place + 4, small * 128 : (small + 1) * 128] = owned_ref[
                g, :, t * 128 : (t + 1) * 128
            ].astype(F32)
    for s in range(8):
        wide_ref[s * 40 + 32 : s * 40 + 40, :] = jnp.zeros((8, 1024), F32)
    rows = rows_ref[...].astype(BF16)
    for h in range(4):
        part = dot(rows, swap_ref[:, h * 256 : (h + 1) * 256], 1, 0)
        for big in range(8):
            for s in range(2):
                place = (h * 2 + s) * 40
                wide_ref[place : place + units, big * 128 : (big + 1) * 128] = part[
                    big * 40 : big * 40 + units, s * 128 : (s + 1) * 128
                ]
    shape = (Q * S, 320)
    r = iota(shape, 0)
    q, s = r // S, r % S
    c, p = q // 2, q % 2
    m = jnp.where(c < 4, p, 2)
    unit = (m * 3 + s // 8) * 4 + jnp.where(c < 4, c, p * 2 + c - 4)
    order = jnp.where(iota(shape, 1) == (s % 8) * 40 + unit, 1.0, 0.0).astype(BF16)
    mine = dot(order, wide_ref[...].astype(BF16), 1, 0).astype(BF16)
    all_ref[...] = mine
    low_ref[...] = mine[: Q * S // 2]
    high_ref[...] = mine[Q * S // 2 :]


PER = 3
DEPTH = 2 * S


def pack_kernel(*refs):
    at = 0
    for ref in refs[:-1]:
        refs[-1][at : at + ref.shape[0]] = ref[...]
        at += ref.shape[0]


def products(first, blocks, c):
    left, other, right = [], [], []
    for ref, base in blocks:
        rows = slice(base + c * DEPTH, base + (c + 1) * DEPTH)
        v = ref[rows, pl.ds(first, 128)].astype(F32)
        left.append(v)
        other += [v[S:], -v[:S]]
        right.append(ref[rows, :])
    left = jnp.concatenate([jnp.concatenate(left, axis=0), jnp.concatenate(other, axis=0)], axis=1)
    return dot(left.astype(BF16), jnp.concatenate(right, axis=0), 0, 0) * (1.0 / (8 * S))


def part_kernel(block_ref, near, rest, near_o, out_ref):
    first = pl.multiple_of(block_ref[0] * 128, 128)
    half = C * DEPTH
    blocks = [(ref, base) for ref in (near, rest, near_o) for base in (0, half)]
    for c in range(C):
        out_ref[c] = products(first, blocks, c)


def last_kernel(block_ref, rest_o, part_ref, out_ref):
    first = pl.multiple_of(block_ref[0] * 128, 128)
    for one in range(PER):
        total = products(first, [(rest_o.at[0], 0), (rest_o.at[1], 0)], one)
        total = total + part_ref[pl.program_id(0) * PER + one]
        out_ref[one] = total.reshape(2, 128, 1024).astype(BF16)


def local(samples, kept):
    block = lax.axis_index("tblk").reshape(1)
    steps = lax.axis_size("tblk")
    tail, channels = pl.pallas_call(
        tail_kernel,
        out_shape=[jax.ShapeDtypeStruct((I, 4, L), BF16), jax.ShapeDtypeStruct((1, kept.shape[0]), F32)],
        in_specs=[VMEM] * 2,
        out_specs=[VMEM] * 2,
        compiler_params=PARAMS,
    )(samples, kept)
    halo = lax.ppermute(tail, "tblk", [(i, i + 1) for i in range(steps - 1)])
    weights = window_table(TAPS, L)
    table, swap = pl.pallas_call(
        table_kernel,
        out_shape=[
            jax.ShapeDtypeStruct((G * Q, L), BF16),
            jax.ShapeDtypeStruct((1024, 1024), BF16),
        ],
        in_specs=[VMEM],
        out_specs=[VMEM, VMEM],
        compiler_params=PARAMS,
        cost_estimate=pl.CostEstimate(flops=10_000_000, bytes_accessed=20_000_000, transcendentals=0),
    )(channels)
    chunks = pl.pallas_call(
        spectra_kernel,
        out_shape=jax.ShapeDtypeStruct((G, 4, 1152), BF16),
        in_specs=[VMEM] * 4,
        out_specs=VMEM,
        scratch_shapes=[pltpu.VMEM((I * S, L), BF16)],
        compiler_params=PARAMS,
    )(table, samples, halo, weights)
    owned = lax.all_to_all(chunks, "inp", split_axis=0, concat_axis=0, tiled=True)
    rows = Q * S
    mine, low, high = pl.pallas_call(
        regroup_kernel,
        out_shape=[jax.ShapeDtypeStruct((n, 1024), BF16) for n in (rows, rows // 2, rows // 2)],
        in_specs=[VMEM] * 2,
        out_specs=[VMEM] * 3,
        scratch_shapes=[pltpu.VMEM((320, 1024), F32), pltpu.VMEM((320, 1024), F32)],
        compiler_params=PARAMS,
    )(owned, swap)
    send = lambda v, hop: lax.ppermute(v, "tblk", [(i, (i + hop) % steps) for i in range(steps)])
    flip = lambda v: lax.ppermute(v, "tblk", [(i, i ^ 1) for i in range(steps)])

    def pack(*parts):
        return pl.pallas_call(
            pack_kernel,
            out_shape=pltpu.VMEM((sum(v.shape[0] for v in parts), 1024), BF16),
            in_specs=[VMEM] * len(parts),
            out_specs=VMEM,
            compiler_params=PARAMS,
        )(*parts)

    up_low, down_high = send(low, 2), send(high, -2)
    up_high, down_low = send(high, 2), send(low, -2)
    far_low, far_high = send(up_low, 2), send(down_high, -2)
    near = pack(mine, up_low, down_high)
    near_o = flip(near)
    rest = pack(down_low, up_high, far_low, far_high)
    rest_o = flip(rest)
    part = pl.pallas_call(
        part_kernel,
        out_shape=pltpu.VMEM((C, 256, 1024), F32),
        in_specs=[pl.BlockSpec(memory_space=pltpu.SMEM)] + [VMEM] * 3,
        out_specs=VMEM,
        compiler_params=PARAMS,
        cost_estimate=pl.CostEstimate(flops=600_000_000, bytes_accessed=9_000_000, transcendentals=0),
    )(block, near, rest, near_o)
    return pl.pallas_call(
        last_kernel,
        out_shape=jax.ShapeDtypeStruct((C, 2, 128, 1024), BF16),
        grid_spec=pltpu.PrefetchScalarGridSpec(
            num_scalar_prefetch=1,
            grid=(C // PER,),
            in_specs=[pl.BlockSpec((2, PER * DEPTH, 1024), lambda c, b: (0, c, 0)), VMEM],
            out_specs=pl.BlockSpec((PER, 2, 128, 1024), lambda c, b: (c, 0, 0, 0)),
        ),
        compiler_params=PARAMS,
    )(block, rest_o.reshape(2, rows, 1024), part)


def solution(mesh):
    placed = (P("inp", "tblk", None), P())
    return jax.shard_map(
        local, mesh=mesh, in_specs=placed, out_specs=P("inp", None, "tblk", None), check_vma=False
    )
```

```python
import math

import jax
import jax.numpy as jnp
from jax import lax
from jax.experimental import pallas as pl
from jax.experimental.pallas import tpu as pltpu
from jax.sharding import PartitionSpec as P

TAPS = 4
L = 2048
G = 64
C = 6
Q = 12
I = 16
S = 24
F32, BF16 = jnp.float32, jnp.bfloat16
PARAMS = pltpu.CompilerParams(vmem_limit_bytes=16 * 1024 * 1024)
VMEM = pl.BlockSpec(memory_space=pltpu.VMEM)


def dot(a, b, ca, cb):
    return lax.dot_general(a, b, (((ca,), (cb,)), ((), ())), preferred_element_type=F32)


def iota(shape, dim):
    return lax.broadcasted_iota(jnp.int32, shape, dim)


def window_table(taps, length_total):
    span = taps * length_total
    t = lax.broadcasted_iota(F32, (taps, length_total), 0)
    m = (taps - 1 - t) * length_total + lax.broadcasted_iota(F32, (taps, length_total), 1)
    return jnp.sinc((m - span / 2.0) / length_total) * (
        0.5 - 0.5 * jnp.cos(2.0 * math.pi * m / span)
    )


def cosine(m):
    r = jnp.abs(((m + L // 2) & (L - 1)) - L // 2)
    flip = r > L // 4
    r = jnp.where(flip, L // 2 - r, r)
    u = r.astype(F32) * (2.0 * math.pi / L)
    u = u * u
    acc = jnp.full_like(u, 1.0 / math.factorial(14) * -1.0)
    for k in range(6, -1, -1):
        acc = acc * u + (-1.0) ** k / math.factorial(2 * k)
    return jnp.where(flip, -acc, acc)


def tail_kernel(samples_ref, kept_ref, out_ref, kept_out):
    out_ref[...] = samples_ref[:, S - 8 :, :].astype(F32)[:, 4:, :].astype(BF16)
    kept_out[...] = kept_ref[...].astype(F32).reshape(1, kept_ref.shape[0])


def table_kernel(kept_ref, table_ref, swap_ref, stripe_ref):
    rows = 2 * G * 4
    r = iota((rows, 1), 0)
    owner = (r // 4) % 2 * (G // 2) + (r // 8) % 32
    tail = r >= G * 4
    want = owner * C + jnp.where(tail, 4 + r % 2, r % 4)
    keep = kept_ref.shape[1]
    chan = jnp.sum(
        jnp.where(iota((rows, keep), 1) == want, kept_ref[...], 0.0), axis=1, keepdims=True
    ).astype(jnp.int32)
    turn = jnp.where(tail, (r // 2) % 2 * (L // 4), 0)
    lane = iota((rows, 128), 1)
    step = chan * 128
    cs = cosine(step + jnp.where(lane < 64, 0, 3 * (L // 4)))
    first = chan * lane + turn
    re0, im0 = cosine(first), cosine(first + 3 * (L // 4))
    half = G * 4
    for n in range(0, rows, 64):
        at = slice(n, n + 64)
        re, im = re0[at], im0[at]
        ca, sa = jnp.broadcast_to(cs[at, 0:1], (64, 128)), jnp.broadcast_to(cs[at, 64:65], (64, 128))
        place = n if n < half else n + half
        for h in range(L // 128):
            cols = slice(h * 128, (h + 1) * 128)
            table_ref[place : place + 64, cols] = re.astype(BF16)
            if n < half:
                table_ref[half + n : half + n + 64, cols] = (-im).astype(BF16)
            re, im = re * ca - im * sa, re * sa + im * ca
    n, lead = 1024, 112
    col = iota((1, 128), 1)
    base = iota((n + lead, 128), 0) - ((col // 16) * 128 + col % 16)
    stripe_ref[...] = jnp.where(base == lead, 1.0, 0.0).astype(BF16)
    for h in range(n // 128):
        at = lead - h * 16
        swap_ref[:, h * 128 : (h + 1) * 128] = stripe_ref[at : at + n, :]


def spectra_kernel(table_ref, samples_ref, halo_ref, weights_ref, out_ref, filtered):
    step = 512

    def fir(pair, carry):
        for n in range(0, L, step):
            cols = slice(n, n + step)
            parts = []
            for one in range(2):
                i = pair * 2 + one
                now = samples_ref[i, :, cols].astype(F32)
                back = halo_ref[i, :, cols].astype(F32)
                frames = jnp.concatenate([back, back, now], axis=0)
                total = weights_ref[0:1, cols] * now
                for d in range(1, TAPS):
                    total = total + weights_ref[d : d + 1, cols] * pltpu.roll(frames, d, 0)[8:]
                parts.append(total)
            both = jnp.concatenate(parts, axis=0).astype(BF16)
            filtered[pl.ds(pl.multiple_of(pair * 2 * S, 2 * S), 2 * S), cols] = both
        return carry

    lax.fori_loop(0, I // 2, fir, 0)
    width = I * S
    col = iota((width, width), 1)
    order = jnp.where(iota((width, width), 0) == (col % I) * S + col // I, 1.0, 0.0).astype(BF16)
    scale = 1.0 / math.sqrt(L)

    def transform(first):
        value = dot(table_ref[first : first + 256, :], filtered[...], 1, 1) * scale
        value = dot(value.astype(BF16), order, 1, 0)
        return value.reshape(32, 8, width)

    for m in range(3):
        value = transform(m * 256).astype(BF16)
        out_ref[0:32, :, m * width : (m + 1) * width] = value[:, 0:4]
        out_ref[32:64, :, m * width : (m + 1) * width] = value[:, 4:8]


def regroup_kernel(owned_ref, swap_ref, all_ref, low_ref, high_ref, rows_ref, wide_ref):
    units = 36
    for g in range(G):
        big, small = g // 8, g % 8
        for t in range(9):
            place = big * 40 + t * 4
            rows_ref[place : place + 4, small * 128 : (small + 1) * 128] = owned_ref[
                g, :, t * 128 : (t + 1) * 128
            ].astype(F32)
    for s in range(8):
        wide_ref[s * 40 + 32 : s * 40 + 40, :] = jnp.zeros((8, 1024), F32)
    rows = rows_ref[...].astype(BF16)
    for h in range(4):
        part = dot(rows, swap_ref[:, h * 256 : (h + 1) * 256], 1, 0)
        for big in range(8):
            for s in range(2):
                place = (h * 2 + s) * 40
                wide_ref[place : place + units, big * 128 : (big + 1) * 128] = part[
                    big * 40 : big * 40 + units, s * 128 : (s + 1) * 128
                ]
    shape = (Q * S, 320)
    r = iota(shape, 0)
    q, s = r // S, r % S
    c, p = q // 2, q % 2
    m = jnp.where(c < 4, p, 2)
    unit = (m * 3 + s // 8) * 4 + jnp.where(c < 4, c, p * 2 + c - 4)
    order = jnp.where(iota(shape, 1) == (s % 8) * 40 + unit, 1.0, 0.0).astype(BF16)
    mine = dot(order, wide_ref[...].astype(BF16), 1, 0).astype(BF16)
    all_ref[...] = mine
    low_ref[...] = mine[: Q * S // 2]
    high_ref[...] = mine[Q * S // 2 :]


PER = 3
DEPTH = 2 * S


def pack_kernel(*refs):
    at = 0
    for ref in refs[:-1]:
        refs[-1][at : at + ref.shape[0]] = ref[...]
        at += ref.shape[0]


def products(first, blocks, c):
    left, other, right = [], [], []
    for ref, base in blocks:
        rows = slice(base + c * DEPTH, base + (c + 1) * DEPTH)
        v = ref[rows, pl.ds(first, 128)].astype(F32)
        left.append(v)
        other += [v[S:], -v[:S]]
        right.append(ref[rows, :])
    left = jnp.concatenate([jnp.concatenate(left, axis=0), jnp.concatenate(other, axis=0)], axis=1)
    return dot(left.astype(BF16), jnp.concatenate(right, axis=0), 0, 0) * (1.0 / (8 * S))


def part_kernel(block_ref, near, rest, near_o, out_ref):
    first = pl.multiple_of(block_ref[0] * 128, 128)
    half = C * DEPTH
    blocks = [(ref, base) for ref in (near, rest, near_o) for base in (0, half)]
    for c in range(C):
        out_ref[c] = products(first, blocks, c)


def last_kernel(block_ref, rest_o, part_ref, out_ref):
    first = pl.multiple_of(block_ref[0] * 128, 128)
    for one in range(PER):
        total = products(first, [(rest_o.at[0], 0), (rest_o.at[1], 0)], one)
        total = total + part_ref[pl.program_id(0) * PER + one]
        out_ref[one] = total.reshape(2, 128, 1024).astype(BF16)


def local(samples, kept):
    block = lax.axis_index("tblk").reshape(1)
    steps = lax.axis_size("tblk")
    tail, channels = pl.pallas_call(
        tail_kernel,
        out_shape=[jax.ShapeDtypeStruct((I, 4, L), BF16), jax.ShapeDtypeStruct((1, kept.shape[0]), F32)],
        in_specs=[VMEM] * 2,
        out_specs=[VMEM] * 2,
        compiler_params=PARAMS,
    )(samples, kept)
    halo = lax.ppermute(tail, "tblk", [(i, i + 1) for i in range(steps - 1)])
    weights = window_table(TAPS, L)
    table, swap = pl.pallas_call(
        table_kernel,
        out_shape=[
            jax.ShapeDtypeStruct((G * Q, L), BF16),
            jax.ShapeDtypeStruct((1024, 1024), BF16),
        ],
        in_specs=[VMEM],
        out_specs=[VMEM, VMEM],
        scratch_shapes=[pltpu.VMEM((1136, 128), BF16)],
        compiler_params=PARAMS,
        cost_estimate=pl.CostEstimate(flops=10_000_000, bytes_accessed=20_000_000, transcendentals=0),
    )(channels)
    chunks = pl.pallas_call(
        spectra_kernel,
        out_shape=jax.ShapeDtypeStruct((G, 4, 1152), BF16),
        in_specs=[VMEM] * 4,
        out_specs=VMEM,
        scratch_shapes=[pltpu.VMEM((I * S, L), BF16)],
        compiler_params=PARAMS,
    )(table, samples, halo, weights)
    owned = lax.all_to_all(chunks, "inp", split_axis=0, concat_axis=0, tiled=True)
    rows = Q * S
    mine, low, high = pl.pallas_call(
        regroup_kernel,
        out_shape=[jax.ShapeDtypeStruct((n, 1024), BF16) for n in (rows, rows // 2, rows // 2)],
        in_specs=[VMEM] * 2,
        out_specs=[VMEM] * 3,
        scratch_shapes=[pltpu.VMEM((320, 1024), F32), pltpu.VMEM((320, 1024), F32)],
        compiler_params=PARAMS,
    )(owned, swap)
    send = lambda v, hop: lax.ppermute(v, "tblk", [(i, (i + hop) % steps) for i in range(steps)])
    flip = lambda v: lax.ppermute(v, "tblk", [(i, i ^ 1) for i in range(steps)])

    def pack(*parts):
        return pl.pallas_call(
            pack_kernel,
            out_shape=pltpu.VMEM((sum(v.shape[0] for v in parts), 1024), BF16),
            in_specs=[VMEM] * len(parts),
            out_specs=VMEM,
            compiler_params=PARAMS,
        )(*parts)

    up_low, down_high = send(low, 2), send(high, -2)
    up_high, down_low = send(high, 2), send(low, -2)
    far_low, far_high = send(up_low, 2), send(down_high, -2)
    near = pack(mine, up_low, down_high)
    near_o = flip(near)
    rest = pack(down_low, up_high, far_low, far_high)
    rest_o = flip(rest)
    part = pl.pallas_call(
        part_kernel,
        out_shape=pltpu.VMEM((C, 256, 1024), F32),
        in_specs=[pl.BlockSpec(memory_space=pltpu.SMEM)] + [VMEM] * 3,
        out_specs=VMEM,
        compiler_params=PARAMS,
        cost_estimate=pl.CostEstimate(flops=600_000_000, bytes_accessed=9_000_000, transcendentals=0),
    )(block, near, rest, near_o)
    return pl.pallas_call(
        last_kernel,
        out_shape=jax.ShapeDtypeStruct((C, 2, 128, 1024), BF16),
        grid_spec=pltpu.PrefetchScalarGridSpec(
            num_scalar_prefetch=1,
            grid=(C // PER,),
            in_specs=[pl.BlockSpec((2, PER * DEPTH, 1024), lambda c, b: (0, c, 0)), VMEM],
            out_specs=pl.BlockSpec((PER, 2, 128, 1024), lambda c, b: (c, 0, 0, 0)),
        ),
        compiler_params=PARAMS,
    )(block, rest_o.reshape(2, rows, 1024), part)


def solution(mesh):
    placed = (P("inp", "tblk", None), P())
    return jax.shard_map(
        local, mesh=mesh, in_specs=placed, out_specs=P("inp", None, "tblk", None), check_vma=False
    )
```
